256 devices in a mesh: ctx: 32 (over x_hi, z, core), row: 4 (over y), col: 2 (over x_lo).
Axes of the slice: x: 4 (x_hi: 2, x_lo: 2; x = x_hi * 2 + x_lo), y: 4, z: 8, core: 2. Of those that a mesh axis runs over, the one named last changes fastest.
Arguments:
- inputs: bfloat16 [4096, 8192], P('ctx', ('row', 'col')), may hold values from -6 to 6
- queries: bfloat16 [4096, 8192], P('ctx', ('row', 'col')), may hold values from -16 to 16
- out_grad: bfloat16 [4096, 8192], P('ctx', ('row', 'col')), may hold values from -6 to 6
- w_key: bfloat16 [8192, 1024], P(('row', 'col')), may hold values from -0.0625 to 0.0625
- w_value: bfloat16 [8192, 1024], P(('row', 'col')), may hold values from -0.0625 to 0.0625
- key_bias: float32 [1024], replicated, may hold values from -16 to 16
- block_order: int32 [64], replicated, may hold values from 0 to 63, as said below
Outputs:
- grad_inputs: bfloat16 [4096, 8192], P('ctx', ('row', 'col'))
- grad_queries: bfloat16 [4096, 8192], P('ctx', ('row', 'col'))
- grad_w_key: bfloat16 [8192, 1024], P(('row', 'col'), 'ctx')
- grad_w_value: bfloat16 [8192, 1024], P(('row', 'col'), 'ctx')
- grad_key_bias: float32 [1024], P('ctx')
- grad_value_bias: float32 [1024], P('ctx')
The draws below stay inside these ranges and needn't reach their ends.
Inputs may be any that keep to these rules, and one draw needn't show every extreme that they name: block_order is a permutation; storage blocks 2 c and 2 c + 1 hold sequence blocks a and 63 - a for some a < 32, in either order.
All inputs are finite; a program needn't handle non-finite values.
Results may differ from the reference program's by a relative error of at most 0.015.
The reference program's roundings to bfloat16 on the way (of `keys`, `values`, `dscore` and `key_low`) count: a program that leaves them out, or rounds other values in their place, can miss the bound.
Values may be sent and summed in bfloat16 or wider, within the bound.
A program may use at most 64 MiB of HBM per device.

```python
import jax
import jax.numpy as jnp
from jax import lax

D = 8192
QH = 64
KVH = 8
HD = 128
BLK = 64
NB = 64
TOKENS = 4096
GROUP = 8
KVD = 1024
QD = 8192


def draw_queries(key, part):
    key = jax.random.fold_in(key, 11)
    key_drawn = jax.random.fold_in(key, 0)
    return jnp.clip(jax.random.normal(key_drawn, (TOKENS, QD), jnp.float32), -16.0, 16.0).astype(jnp.bfloat16)


def draw_key_bias(key, part):
    key = jax.random.fold_in(key, 23)
    key_big = jax.random.fold_in(key, 0)
    return jnp.clip(0.5 * jax.random.normal(key_big, (KVD,), jnp.float32), -16.0, 16.0)


def draw_block_order(key, part):
    key = jax.random.fold_in(key, 37)
    key_perm, key_flip = jax.random.split(key)
    pair_count = NB // 2
    low_blocks = jax.random.permutation(key_perm, pair_count).astype(jnp.int32)
    flip_bits = jax.random.randint(key_flip, (pair_count,), 0, 2).astype(jnp.int32)
    high_blocks = (NB - 1 - low_blocks).astype(jnp.int32)
    first_slot = jnp.where(flip_bits == 1, high_blocks, low_blocks)
    second = jnp.where(flip_bits == 1, low_blocks, high_blocks)
    return jnp.stack([first_slot, second], axis=1).reshape(NB).astype(jnp.int32)


def block_scale(key, dims, cuts, least, top_value):
    def one(dim, parts):
        draws = jax.random.uniform(jax.random.fold_in(jax.random.fold_in(key, 6), dim), (parts,), jnp.float32, least / len(cuts), top_value / len(cuts))
        return jnp.repeat(jnp.exp(draws), dims[dim] // parts).reshape((-1,) + (1,) * (len(dims) - dim - 1))

    gain = one(*cuts[0])
    for cut in cuts[1:]:
        gain = gain * one(*cut)
    return gain


def normal_values(stream_key, dims, deviation, bound, cuts=(), held_as=jnp.bfloat16):
    array = deviation * jax.random.normal(stream_key, dims, jnp.float32)
    if cuts:
        array = array * block_scale(stream_key, dims, cuts, -0.22, 0.18)
    return jnp.clip(array, -bound, bound).astype(held_as)


def setup_inputs(seed: int = 0) -> dict:
    streams_of = jax.random.split(jax.random.key(seed), 8)
    inputs = normal_values(streams_of[0], (TOKENS, D), 1.0, 6.0, ((0, 32), (1, 8)))
    queries = draw_queries(jax.random.fold_in(streams_of[7], 71), 0)
    out_grad = normal_values(streams_of[2], (TOKENS, QD), 1.0, 6.0, ((0, 32), (1, 8)))
    w_key = normal_values(streams_of[3], (D, KVD), D ** -0.5, 0.0625, ((0, 8),))
    w_value = normal_values(streams_of[4], (D, KVD), D ** -0.5, 0.0625, ((0, 8),))
    key_bias = draw_key_bias(jax.random.fold_in(streams_of[7], 71), 0)
    block_order = draw_block_order(jax.random.fold_in(streams_of[7], 71), 0)
    return dict(inputs=inputs, queries=queries, out_grad=out_grad, w_key=w_key, w_value=w_value, key_bias=key_bias, block_order=block_order)


ROPE_BASE = 1000000.0
MASKED = -1e30


def rope_tables(positions):
    half_width = HD // 2
    frequency = ROPE_BASE ** (-jnp.arange(half_width, dtype=jnp.float32) * 2.0 / HD)
    angles = positions.astype(jnp.float32)[:, None] * frequency[None, :]
    return jnp.cos(angles), jnp.sin(angles)


def rotate(tensor, cosine_table, sine_table):
    half_width = tensor.shape[-1] // 2
    lower_part = tensor[..., :half_width]
    upper_part = tensor[..., half_width:]
    return jnp.concatenate([lower_part * cosine_table - upper_part * sine_table, upper_part * cosine_table + lower_part * sine_table], axis=-1)


def unrotate(tensor, cosine_table, sine_table):
    half_width = tensor.shape[-1] // 2
    lower_part = tensor[..., :half_width]
    upper_part = tensor[..., half_width:]
    return jnp.concatenate([lower_part * cosine_table + upper_part * sine_table, upper_part * cosine_table - lower_part * sine_table], axis=-1)


def reference(inputs, queries, out_grad, w_key, w_value, key_bias, block_order):
    row_ids = jnp.arange(TOKENS, dtype=jnp.int32)
    positions = (block_order[row_ids // BLK] * BLK + row_ids % BLK).astype(jnp.int32)
    cosine_table, sine_table = rope_tables(positions)
    key_pre = jnp.dot(inputs, w_key, preferred_element_type=jnp.float32) + key_bias
    keys = rotate(key_pre.reshape(TOKENS, KVH, HD), cosine_table[:, None, :], sine_table[:, None, :]).astype(jnp.bfloat16)
    values = jnp.dot(inputs, w_value, preferred_element_type=jnp.float32).reshape(TOKENS, KVH, HD).astype(jnp.bfloat16)
    keys_heads = keys.transpose(1, 0, 2)
    values_heads = values.transpose(1, 0, 2)
    query_heads = queries.reshape(TOKENS, QH, HD).transpose(1, 0, 2)
    grad_heads = out_grad.reshape(TOKENS, QH, HD).transpose(1, 0, 2)
    owners = (jnp.arange(QH, dtype=jnp.int32) // GROUP).astype(jnp.int32)
    block_rows = min(TOKENS, 1024)
    block_count = TOKENS // block_rows
    score_scale = HD ** -0.5
    pos_blocks = positions.reshape(block_count, block_rows)

    def one_head(operands):
        query_head, gradient, owner_index = operands
        head_keys = lax.dynamic_index_in_dim(keys_heads, owner_index, 0, keepdims=False)
        head_values = lax.dynamic_index_in_dim(values_heads, owner_index, 0, keepdims=False)

        def one_block(running, pieces):
            key_acc, value_acc = running
            query_block, grad_block, pos_block = pieces
            scores = jnp.dot(query_block, head_keys.T, preferred_element_type=jnp.float32) * score_scale
            visible = positions[None, :] <= pos_block[:, None]
            scores = jnp.where(visible, scores, MASKED)
            row_top = jnp.max(scores, axis=1, keepdims=True)
            row_total = jnp.sum(jnp.where(visible, jnp.exp(scores - row_top), 0.0), axis=1, keepdims=True)
            log_total = row_top + jnp.log(row_total)
            probability = jnp.where(visible, jnp.exp(scores - log_total), 0.0)
            grad_prob = jnp.dot(grad_block, head_values.T, preferred_element_type=jnp.float32)
            delta_rows = jnp.sum(probability * grad_prob, axis=1, keepdims=True)
            dscore = (probability * (grad_prob - delta_rows)).astype(jnp.bfloat16)
            prob_low = probability.astype(jnp.bfloat16)
            dquery = (jnp.dot(dscore, head_keys, preferred_element_type=jnp.float32) * score_scale).astype(jnp.bfloat16)
            key_acc = key_acc + jnp.dot(dscore.T, query_block, preferred_element_type=jnp.float32) * score_scale
            value_acc = value_acc + jnp.dot(prob_low.T, grad_block, preferred_element_type=jnp.float32)
            return (key_acc, value_acc), dquery

        zero_rows = jnp.zeros((TOKENS, HD), jnp.float32)
        pieces = (query_head.reshape(block_count, block_rows, HD), gradient.reshape(block_count, block_rows, HD), pos_blocks)
        (key_acc, value_acc), dquery = lax.scan(one_block, (zero_rows, zero_rows), pieces)
        return dquery.reshape(TOKENS, HD), key_acc, value_acc

    dquery, key_grad, value_grad = lax.map(one_head, (query_heads, grad_heads, owners))
    key_grad = key_grad.reshape(KVH, GROUP, TOKENS, HD).sum(axis=1).transpose(1, 0, 2)
    value_grad = value_grad.reshape(KVH, GROUP, TOKENS, HD).sum(axis=1).transpose(1, 0, 2)
    key_grad_pre = unrotate(key_grad, cosine_table[:, None, :], sine_table[:, None, :]).reshape(TOKENS, KVD)
    value_flat = value_grad.reshape(TOKENS, KVD)
    key_low = key_grad_pre.astype(jnp.bfloat16)
    value_low = value_flat.astype(jnp.bfloat16)
    grad_inputs = (jnp.dot(key_low, w_key.T, preferred_element_type=jnp.float32) + jnp.dot(value_low, w_value.T, preferred_element_type=jnp.float32)).astype(jnp.bfloat16)
    grad_queries = dquery.transpose(1, 0, 2).reshape(TOKENS, QD)
    grad_w_key = jnp.dot(inputs.T, key_low, preferred_element_type=jnp.float32).astype(jnp.bfloat16)
    grad_w_value = jnp.dot(inputs.T, value_low, preferred_element_type=jnp.float32).astype(jnp.bfloat16)
    grad_key_bias = jnp.sum(key_grad_pre, axis=0)
    grad_value_bias = jnp.sum(value_flat, axis=0)
    return grad_inputs, grad_queries, grad_w_key, grad_w_value, grad_key_bias, grad_value_bias
```

```python
import functools
import math

import jax
import jax.numpy as jnp
import numpy as np
from jax import lax
from jax.experimental import pallas as pl
from jax.experimental.pallas import tpu as pltpu
from jax.sharding import PartitionSpec as P

HD = 128
ROPE_BASE = 1000000.0
MASKED = -1e30
F32 = jnp.float32
BF16 = jnp.bfloat16
SCALE = HD ** -0.5
LOG2E = math.log2(math.e)
MESH = pl.DeviceIdType.MESH
VMEM = pltpu.VMEM

NCTX = 32
NZ = 8
NROW = 4
NCOL = 2
NHEAD = 8
TOK = 128
BLK = 64
TILE = 256
SEQ = NCTX * TOK
ROWS = 8 * BLK
MODEL = 1024
HEAD_STEPS = ((2, 1), (2, 0), (1, 1), (3, 1), (1, 0), (3, 0), (0, 1))


class Place:
    def __init__(self):
        self.ctx = lax.axis_index("ctx")
        self.row = lax.axis_index("row")
        self.col = lax.axis_index("col")
        self.core = lax.rem(self.ctx, 2)
        self.z = lax.rem(lax.div(self.ctx, 2), NZ)
        self.xh = lax.div(self.ctx, 2 * NZ)
        self.head = self.row * NCOL + self.col

    def slot(self, xh, z, core):
        return (xh * NZ + lax.rem(z + 2 * NZ, NZ)) * 2 + core

    def ctx_device(self, xh, z, core):
        return (self.slot(xh, z, core), self.row, self.col)

    def right(self):
        return self.ctx_device(self.xh, self.z + 1, self.core)

    def left(self):
        return self.ctx_device(self.xh, self.z - 1, self.core)

    def across(self):
        return self.ctx_device(1 - self.xh, self.z, self.core)

    def sibling(self):
        return self.ctx_device(self.xh, self.z, 1 - self.core)

    def head_peer(self, step):
        row = lax.rem(self.row + step[0], NROW)
        col = lax.rem(self.col + step[1], NCOL)
        return row, col

    def head_device(self, step):
        row, col = self.head_peer(step)
        return (self.ctx, row, col)

    def head_source(self, step):
        row = lax.rem(self.row + NROW - step[0], NROW)
        col = lax.rem(self.col + NCOL - step[1], NCOL)
        return row * NCOL + col

    def greet(self):
        barrier = pltpu.get_barrier_semaphore()
        others = [self.right(), self.left(), self.across(), self.sibling()]
        others += [self.head_device(step) for step in HEAD_STEPS]
        for device in others:
            pl.semaphore_signal(barrier, inc=1, device_id=device, device_id_type=MESH)
        pl.semaphore_wait(barrier, len(others))


def remote(src, dst, send_sem, recv_sem, device):
    return pltpu.make_async_remote_copy(
        src_ref=src,
        dst_ref=dst,
        send_sem=send_sem,
        recv_sem=recv_sem,
        device_id=device,
        device_id_type=MESH,
    )


def turned(tensor):
    return jnp.concatenate([tensor[:, HD // 2 :], tensor[:, : HD // 2]], axis=1)


def gather_kernel(
    x_ref, wk_ref, wv_ref, bias_ref, cos_ref, sin_ref, kv_ref,
    part_k, part_v, got_k, got_v, ks, kr, vs, vr, ring_send, ring_recv,
):
    me = Place()
    me.greet()
    x = x_ref[...]
    sends = []

    def partial(head):
        columns = pl.ds(pl.multiple_of(head * HD, HD), HD)
        return (
            jnp.dot(x, wk_ref[:, columns], preferred_element_type=F32),
            jnp.dot(x, wv_ref[:, columns], preferred_element_type=F32),
        )

    for i, step in enumerate(HEAD_STEPS):
        row, col = me.head_peer(step)
        key, value = partial(row * NCOL + col)
        part_k[i] = key.astype(part_k.dtype)
        part_v[i] = value.astype(part_v.dtype)
        device = (me.ctx, row, col)
        for part, got, ss, rs in ((part_k, got_k, ks, kr), (part_v, got_v, vs, vr)):
            copy = remote(part.at[i], got.at[i], ss.at[i], rs.at[i], device)
            copy.start()
            sends.append(copy)
    key, value = partial(me.head)
    key = key + bias_ref[pl.ds(me.head, 1), :]
    for i in range(len(HEAD_STEPS)):
        sends[2 * i].wait_recv()
        key = key + got_k[i].astype(F32)
        sends[2 * i + 1].wait_recv()
        value = value + got_v[i].astype(F32)
    own = me.slot(me.xh, me.z, me.core)
    kv_ref[own, 0] = (key * cos_ref[...] + turned(key) * sin_ref[...]).astype(BF16)
    kv_ref[own, 1] = value.astype(BF16)

    targets = (me.right(), me.left(), me.across(), me.sibling())

    def pass_on(slot, directions):
        for way in directions:
            copy = remote(
                kv_ref.at[slot], kv_ref.at[slot], ring_send.at[way, slot], ring_recv.at[slot], targets[way]
            )
            copy.start()
            sends.append(copy)

    def arrived(slot):
        remote(
            kv_ref.at[slot], kv_ref.at[slot], ring_send.at[0, slot], ring_recv.at[slot], targets[3]
        ).wait_recv()

    R, L, X, C = range(4)
    pass_on(own, (R, L, X, C))
    here, there = me.xh, 1 - me.xh
    plan = (
        (here, -1, (R, C)), (here, 1, (L, C)),
        (there, 0, (R, L, C)),
        (here, -2, (R, C)), (here, 2, (L, C)),
        (there, -1, (R, C)), (there, 1, (L, C)),
        (here, -3, (R, C)), (here, 3, (C,)),
        (there, -2, (R, C)), (there, 2, (L, C)),
        (here, -4, (C,)),
        (there, -3, (C,)), (there, 3, (L, C)),
        (there, 4, (C,)),
    )
    for xh, dz, ways in plan:
        slot = me.slot(xh, me.z + dz, me.core)
        arrived(slot)
        pass_on(slot, ways)
    arrived(me.slot(here, me.z, 1 - me.core))
    for xh, dz, _ in plan:
        arrived(me.slot(xh, me.z + dz, 1 - me.core))
    for copy in sends:
        copy.wait_send()


def gather_keys(x, w_key, w_value, bias, cos, sin):
    steps = len(HEAD_STEPS)
    vmem = pl.BlockSpec(memory_space=VMEM)
    dma = pltpu.SemaphoreType.DMA
    return pl.pallas_call(
        gather_kernel,
        name="project_gather",
        out_shape=jax.ShapeDtypeStruct((NCTX, 2, TOK, HD), BF16),
        in_specs=[vmem] * 6,
        out_specs=vmem,
        scratch_shapes=[
            VMEM((steps, TOK, HD), F32),
            VMEM((steps, TOK, HD), BF16),
            VMEM((steps, TOK, HD), F32),
            VMEM((steps, TOK, HD), BF16),
            dma((steps,)), dma((steps,)), dma((steps,)), dma((steps,)),
            dma((4, NCTX)), dma((NCTX,)),
        ],
        compiler_params=pltpu.CompilerParams(
            collective_id=0, has_side_effects=True, vmem_limit_bytes=40 * 2**20
        ),
    )(x, w_key, w_value, bias, cos, sin)


def attend_kernel(
    order_ref, q_ref, g_ref, kv_ref, dq_ref, dkv_ref,
    keys, values, rows_q, rows_g, cols_q, cols_g, sum_k, sum_v, sum_q,
):
    ctx = lax.axis_index("ctx")
    first, second = order_ref[2 * ctx], order_ref[2 * ctx + 1]
    low_half = jnp.where(first < second, 0, 1)
    low_block = jnp.minimum(first, second)
    high_block = jnp.maximum(first, second)

    def collect(i, carry):
        for half in range(2):
            block = order_ref[2 * i + half]
            to = pl.ds(pl.multiple_of(block * BLK, BLK), BLK)
            keys[to, :] = kv_ref[i, 0, half * BLK : (half + 1) * BLK, :]
            values[to, :] = kv_ref[i, 1, half * BLK : (half + 1) * BLK, :]
        return carry

    lax.fori_loop(0, NCTX, collect, 0)
    for half in range(2):
        index = jnp.where(low_half == half, 1, 0)
        for head in range(8):
            place = (slice(half * BLK, (half + 1) * BLK), slice(head * HD, (head + 1) * HD))
            rows_q[index, head * BLK : (head + 1) * BLK, :] = q_ref[place]
            rows_g[index, head * BLK : (head + 1) * BLK, :] = g_ref[place]
    for index in range(2):
        cols_q[index] = rows_q[index].T
        cols_g[index] = rows_g[index].T

    step = (
        lax.broadcasted_iota(jnp.int32, (TILE, ROWS), 0)
        - lax.broadcasted_iota(jnp.int32, (TILE, ROWS), 1) % BLK
    )
    blocks = (high_block, low_block)

    def tile_scores(index, tile, masked):
        here = pl.ds(pl.multiple_of(tile * TILE, TILE), TILE)
        key, value = keys[here, :], values[here, :]
        score = jnp.dot(key, cols_q[index], preferred_element_type=F32) * (SCALE * LOG2E)
        grad = jnp.dot(value, cols_g[index], preferred_element_type=F32)
        if masked:
            visible = step <= blocks[index] * BLK - tile * TILE
            score = jnp.where(visible, score, MASKED)
        return here, key, score, grad

    for index in range(2):
        last = blocks[index] // (TILE // BLK)

        def totals(tile, state, masked=False):
            top, total, weighted = state
            _, _, score, grad = tile_scores(index, tile, masked)
            new_top = jnp.maximum(top, jnp.max(score, axis=0, keepdims=True))
            prob = jnp.exp2(score - new_top)
            rescale = jnp.exp2(top - new_top)
            total = total * rescale + jnp.sum(prob, axis=0, keepdims=True)
            weighted = weighted * rescale + jnp.sum(prob * grad, axis=0, keepdims=True)
            return new_top, total, weighted

        zero = jnp.zeros((1, ROWS), F32)
        state = (jnp.full((1, ROWS), MASKED, F32), zero, zero)
        state = lax.fori_loop(0, last, totals, state)
        top, total, weighted = totals(last, state, masked=True)
        log_total = top + jnp.log2(total)
        delta = weighted / total
        sum_q[...] = jnp.zeros_like(sum_q)

        def gradients(tile, masked=False):
            here, key, score, grad = tile_scores(index, tile, masked)
            prob = jnp.exp2(score - log_total)
            dscore = (prob * (grad - delta)).astype(BF16)
            prob_low = prob.astype(BF16)
            key_term = jnp.dot(dscore, rows_q[index], preferred_element_type=F32)
            value_term = jnp.dot(prob_low, rows_g[index], preferred_element_type=F32)
            if index == 0:
                sum_k[here, :] = key_term
                sum_v[here, :] = value_term
            else:
                sum_k[here, :] += key_term
                sum_v[here, :] += value_term
            sum_q[...] += jnp.dot(key.T, dscore, preferred_element_type=F32)

        @pl.loop(0, last)
        def _(tile):
            gradients(tile)

        gradients(last, masked=True)
        if index == 0:

            @pl.loop(last + 1, SEQ // TILE)
            def _(tile):
                here = pl.ds(pl.multiple_of(tile * TILE, TILE), TILE)
                sum_k[here, :] = jnp.zeros((TILE, HD), F32)
                sum_v[here, :] = jnp.zeros((TILE, HD), F32)

        query = (sum_q[...] * SCALE).T.astype(BF16)
        half = low_half if index == 1 else 1 - low_half
        to = pl.ds(pl.multiple_of(half * BLK, BLK), BLK)
        for head in range(8):
            dq_ref[to, head * HD : (head + 1) * HD] = query[head * BLK : (head + 1) * BLK, :]

    def spread(i, carry):
        core, z, xh = lax.rem(i, 2), lax.rem(lax.div(i, 2), NZ), lax.div(i, 2 * NZ)
        for half in range(2):
            block = order_ref[2 * i + half]
            src = pl.ds(pl.multiple_of(block * BLK, BLK), BLK)
            rows = slice(half * BLK, (half + 1) * BLK)
            dkv_ref[core, z, xh, 0, rows, :] = (sum_k[src, :] * SCALE).astype(BF16)
            dkv_ref[core, z, xh, 1, rows, :] = sum_v[src, :].astype(BF16)
        return carry

    lax.fori_loop(0, NCTX, spread, 0)


def attend(order, queries, out_grad, kv):
    vmem = pl.BlockSpec(memory_space=VMEM)
    return pl.pallas_call(
        attend_kernel,
        name="attend",
        out_shape=(
            jax.ShapeDtypeStruct((TOK, MODEL), BF16),
            jax.ShapeDtypeStruct((2, NZ, 2, 2, TOK, HD), BF16),
        ),
        in_specs=[pl.BlockSpec(memory_space=pltpu.SMEM), vmem, vmem, vmem],
        out_specs=(vmem, vmem),
        scratch_shapes=[
            VMEM((SEQ, HD), BF16), VMEM((SEQ, HD), BF16),
            VMEM((2, ROWS, HD), BF16), VMEM((2, ROWS, HD), BF16),
            VMEM((2, HD, ROWS), BF16), VMEM((2, HD, ROWS), BF16),
            VMEM((SEQ, HD), F32), VMEM((SEQ, HD), F32),
            VMEM((HD, ROWS), F32),
        ],
        compiler_params=pltpu.CompilerParams(vmem_limit_bytes=40 * 2**20),
    )(order, queries, out_grad, kv)


RIGHT_FROM = (4, 3)
LEFT_FROM = (3, 4)
ORDER = (4, 3, 5, 2, 6, 1, 7, 0)


class Ring:
    def __init__(self, me, send, recv, cross, send_sem, recv_sem, cross_send, cross_recv, mine):
        self.me, self.send, self.recv, self.cross = me, send, recv, cross
        self.send_sem, self.recv_sem = send_sem, recv_sem
        self.cross_send, self.cross_recv = cross_send, cross_recv
        self.mine = mine
        self.copies = {}

    def sends(self, p, way, distance):
        i = p * 7 + (distance - 1 if way == 0 else RIGHT_FROM[p] + distance - 1)
        begin = (RIGHT_FROM if way == 0 else LEFT_FROM)[p]
        term = self.mine(p, distance if way == 0 else NZ - distance)
        if distance < begin:
            term = term + self.take(p, way, distance + 1)
        self.send[i] = term.astype(self.send.dtype)
        device = self.me.right() if way == 0 else self.me.left()
        copy = remote(
            self.send.at[i], self.recv.at[i], self.send_sem.at[i], self.recv_sem.at[i], device
        )
        copy.start()
        self.copies[p, way, distance] = copy, i

    def take(self, p, way, distance):
        copy, i = self.copies[p, way, distance]
        copy.wait_recv()
        return self.recv[i].astype(F32)

    def finish_other(self):
        term = self.mine(1, 0) + self.take(1, 0, 1) + self.take(1, 1, 1)
        self.cross[0] = term.astype(self.cross.dtype)
        self.cross_copy = remote(
            self.cross.at[0], self.cross.at[1], self.cross_send, self.cross_recv, self.me.across()
        )
        self.cross_copy.start()

    def finish_own(self):
        term = self.mine(0, 0) + self.take(0, 0, 1) + self.take(0, 1, 1)
        self.cross_copy.wait_recv()
        return term + self.cross[1].astype(F32)

    def drain(self):
        for copy, _ in self.copies.values():
            copy.wait_send()
        self.cross_copy.wait_send()


RING_ROUNDS = (
    ((0, 0, 4), (1, 1, 4)),
    ((1, 0, 3), (0, 1, 3)),
    ((0, 0, 3), (1, 1, 3)),
    ((1, 0, 2), (0, 1, 2)),
    ((0, 0, 2), (1, 1, 2)),
    ((1, 0, 1), (0, 1, 1)),
    ((1, 1, 1), (0, 0, 1)),
)


def finish_kernel(
    x_ref, wk_hbm, wv_hbm, cos_ref, sin_ref, dkv_ref,
    gx_ref, gw_ref, gb_ref,
    wk, wv, both_x, pair, low, low_pair, bias, bias_pair, terms,
    send_a, recv_a, cross_a, send_b, recv_b, cross_b, send_c, recv_c, cross_c,
    w_sem, x_sem, pair_send, pair_recv, low_send, low_recv, bias_send, bias_recv,
    fwd_send, fwd_recv, sems_a, sems_b, sems_c, cross_sems,
):
    me = Place()
    load_k = pltpu.make_async_copy(wk_hbm, wk, w_sem.at[0])
    load_v = pltpu.make_async_copy(wv_hbm, wv, w_sem.at[1])
    load_k.start()
    load_v.start()
    me.greet()
    sibling = me.sibling()
    core, other = me.core, 1 - me.core

    def along(dz):
        return lax.rem(me.z + dz, NZ)

    pair_copies = {}
    for dz in ORDER:
        z = along(dz)
        copy = remote(dkv_ref.at[other, z], pair.at[z], pair_send.at[z], pair_recv.at[z], sibling)
        copy.start()
        pair_copies[dz] = copy
    share_x = remote(x_ref, both_x.at[1], x_sem.at[0], x_sem.at[1], sibling)
    share_x.start()
    both_x[0] = x_ref[...]
    seen = set()

    def side(p):
        return me.xh if p == 0 else 1 - me.xh

    def mine_a(p, dz):
        if dz not in seen:
            pair_copies[dz].wait_recv()
            seen.add(dz)
        z = along(dz)
        return dkv_ref[core, z, side(p)].astype(F32) + pair[z, side(p)].astype(F32)

    ring = Ring(
        me, send_a, recv_a, cross_a, sems_a.at[0], sems_a.at[1], cross_sems.at[0], cross_sems.at[1], mine_a
    )
    for group in RING_ROUNDS:
        for item in group:
            ring.sends(*item)
    ring.finish_other()
    total = ring.finish_own()
    key, value = total[0], total[1]
    key = key * cos_ref[...] - turned(key) * sin_ref[...]
    low[me.head, 0] = key.T.astype(BF16)
    low[me.head, 1] = value.T.astype(BF16)
    key_sum = jnp.sum(key, axis=0, keepdims=True)
    value_sum = jnp.sum(value, axis=0, keepdims=True)
    line = lax.broadcasted_iota(jnp.int32, (8, HD), 0)
    bias[me.head] = jnp.where(line == 0, key_sum, jnp.where(line == 1, value_sum, 0.0))

    copies = []
    for i, step in enumerate(HEAD_STEPS):
        device = me.head_device(step)
        for array, ss, rs in ((low, low_send, low_recv), (bias, bias_send, bias_recv)):
            copy = remote(array.at[me.head], array.at[me.head], ss.at[i], rs.at[i], device)
            copy.start()
            copies.append(copy)

    forwards = []

    def forward(head, i):
        copy = remote(low.at[head], low_pair.at[head], fwd_send.at[i], fwd_recv.at[i], sibling)
        copy.start()
        forwards.append(copy)

    forward(me.head, 7)
    for i in (6, 4, 5, 2, 3, 1, 0):
        source = me.head_source(HEAD_STEPS[i])
        remote(low.at[source], low.at[source], low_send.at[i], low_recv.at[i], sibling).wait_recv()
        forward(source, i)
    for i in range(7):
        copies[2 * i + 1].wait_recv()
    share_bias = remote(bias, bias_pair, x_sem.at[2], x_sem.at[3], sibling)
    share_bias.start()
    share_x.wait_recv()
    for copy in forwards:
        copy.wait_recv()

    tokens = both_x[...].reshape(2 * TOK, MODEL)

    def chip_rows(z, xh):
        chip = xh * NZ + z
        head, half = lax.div(chip, 2), lax.rem(chip, 2)
        rows = pl.ds(pl.multiple_of(half * 64 + core * 32, 32), 32)
        return jnp.concatenate(
            [
                jnp.concatenate([low[head, part, rows, :], low_pair[head, part, rows, :]], axis=1)
                for part in range(2)
            ],
            axis=0,
        )

    def weigh(dz):
        z = along(dz)
        left = jnp.concatenate([chip_rows(z, side(0)), chip_rows(z, side(1))], axis=0)
        out = jnp.dot(left, tokens, preferred_element_type=F32)
        terms[dz] = out.reshape(2, 64, MODEL)

    def mine_b(p, dz):
        return terms[dz, p]

    def mine_c(p, dz):
        head = lax.div(side(p) * NZ + along(dz), 2)
        return bias[head] + bias_pair[head]

    ring_b = Ring(
        me, send_b, recv_b, cross_b, sems_b.at[0], sems_b.at[1], cross_sems.at[2], cross_sems.at[3], mine_b
    )
    ring_c = Ring(
        me, send_c, recv_c, cross_c, sems_c.at[0], sems_c.at[1], cross_sems.at[4], cross_sems.at[5], mine_c
    )

    def both(group):
        for item in group:
            ring_b.sends(*item)
        for item in group:
            ring_c.sends(*item)

    weigh(4)
    for item in RING_ROUNDS[0]:
        ring_b.sends(*item)
    weigh(3)
    weigh(5)
    for item in RING_ROUNDS[1]:
        ring_b.sends(*item)
    share_bias.wait_recv()
    for group in RING_ROUNDS[:2]:
        for item in group:
            ring_c.sends(*item)
    for dz in (2, 6, 1, 7, 0):
        weigh(dz)
    both(RING_ROUNDS[2])
    load_k.wait()
    load_v.wait()
    low_key = low[:, 0].reshape(NHEAD * HD, TOK)
    low_value = low[:, 1].reshape(NHEAD * HD, TOK)
    gx = jnp.dot(wk[...], low_key, preferred_element_type=F32)
    gx = gx + jnp.dot(wv[...], low_value, preferred_element_type=F32)
    gx_ref[...] = gx.T.astype(BF16)
    for group in RING_ROUNDS[3:]:
        both(group)
    ring_b.finish_other()
    ring_c.finish_other()
    gw_ref[...] = ring_b.finish_own().astype(BF16)
    gb_ref[...] = ring_c.finish_own()

    for copy in pair_copies.values():
        copy.wait_send()
    share_x.wait_send()
    share_bias.wait_send()
    for copy in copies + forwards:
        copy.wait_send()
    ring.drain()
    ring_b.drain()
    ring_c.drain()


def finish(x, w_key, w_value, cos, sin, dkv):
    vmem = pl.BlockSpec(memory_space=VMEM)
    hbm = pl.BlockSpec(memory_space=pl.ANY)
    dma = pltpu.SemaphoreType.DMA
    return pl.pallas_call(
        finish_kernel,
        name="finish",
        out_shape=(
            jax.ShapeDtypeStruct((TOK, MODEL), BF16),
            jax.ShapeDtypeStruct((64, MODEL), BF16),
            jax.ShapeDtypeStruct((8, HD), F32),
        ),
        in_specs=[vmem, hbm, hbm, vmem, vmem, vmem],
        out_specs=(vmem, vmem, vmem),
        scratch_shapes=[
            VMEM((MODEL, NHEAD * HD), BF16), VMEM((MODEL, NHEAD * HD), BF16),
            VMEM((2, TOK, MODEL), BF16),
            VMEM((NZ, 2, 2, TOK, HD), BF16),
            VMEM((NHEAD, 2, HD, TOK), BF16), VMEM((NHEAD, 2, HD, TOK), BF16),
            VMEM((NHEAD, 8, HD), F32), VMEM((NHEAD, 8, HD), F32),
            VMEM((NZ, 2, 64, MODEL), F32),
            VMEM((14, 2, TOK, HD), BF16), VMEM((14, 2, TOK, HD), BF16), VMEM((2, 2, TOK, HD), BF16),
            VMEM((14, 64, MODEL), BF16), VMEM((14, 64, MODEL), BF16), VMEM((2, 64, MODEL), BF16),
            VMEM((14, 8, HD), F32), VMEM((14, 8, HD), F32), VMEM((2, 8, HD), F32),
            dma((2,)), dma((4,)), dma((NZ,)), dma((NZ,)),
            dma((7,)), dma((7,)), dma((7,)), dma((7,)),
            dma((8,)), dma((8,)),
            dma((2, 14)), dma((2, 14)), dma((2, 14)), dma((6,)),
        ],
        compiler_params=pltpu.CompilerParams(
            collective_id=1, has_side_effects=True, vmem_limit_bytes=50 * 2**20
        ),
    )(x, w_key, w_value, cos, sin, dkv)


def rope_tables(order):
    frequency = (ROPE_BASE ** (-np.arange(HD // 2) * 2.0 / HD)).astype(np.float32)
    pair = lax.dynamic_slice_in_dim(order, 2 * lax.axis_index("ctx"), 2)
    positions = (pair[:, None] * BLK + jnp.arange(BLK, dtype=jnp.int32)[None, :]).reshape(TOK)
    angles = positions.astype(F32)[:, None] * jnp.asarray(frequency)[None, :]
    cos, sin = jnp.cos(angles), jnp.sin(angles)
    return jnp.concatenate([cos, cos], axis=1), jnp.concatenate([-sin, sin], axis=1)


def body(inputs, queries, out_grad, w_key, w_value, key_bias, block_order):
    cos, sin = rope_tables(block_order)
    kv = gather_keys(inputs, w_key, w_value, key_bias.reshape(NHEAD, HD), cos, sin)
    grad_queries, dkv = attend(block_order, queries, out_grad, kv)
    grad_inputs, grad_w, grad_b = finish(inputs, w_key, w_value, cos, sin, dkv)
    start = lax.rem(lax.axis_index("ctx"), 4) * 32
    grad_b = lax.dynamic_slice(grad_b, (0, start), (2, 32))
    return grad_inputs, grad_queries, grad_w[:32].T, grad_w[32:].T, grad_b[0], grad_b[1]


def solution(mesh):
    return jax.shard_map(
        body,
        mesh=mesh,
        in_specs=(
            P("ctx", ("row", "col")),
            P("ctx", ("row", "col")),
            P("ctx", ("row", "col")),
            P(("row", "col"), None),
            P(("row", "col"), None),
            P(),
            P(),
        ),
        out_specs=(
            P("ctx", ("row", "col")),
            P("ctx", ("row", "col")),
            P(("row", "col"), "ctx"),
            P(("row", "col"), "ctx"),
            P("ctx"),
            P("ctx"),
        ),
        check_vma=False,
    )
```
